256 devices in a mesh: dp: 4 (over y), expert: 8 (over x, z_hi), cuts: 8 (over z_lo, core).
Axes of the slice: x: 4, y: 4, z: 8 (z_hi: 2, z_lo: 4; z = z_hi * 4 + z_lo), core: 2. Of those that a mesh axis runs over, the one named last changes fastest.
Arguments:
- tokens: bfloat16 [4096, 3072], P(('dp', 'expert'), 'cuts'), may hold values from -6 to 6
- cotangent: bfloat16 [4096, 3072], P(('dp', 'expert'), 'cuts'), may hold values from -6 to 6
- combine: float32 [4096, 2], P(('dp', 'expert')), may hold values from 0.25 to 1
- expert_ids: int32 [4096, 2], P(('dp', 'expert')), may hold values from 0 to 7, as said below
- slot_ids: int32 [4096, 2], P(('dp', 'expert')), may hold values from 0 to 35, as said below
- keep_mask: int32 [4096, 2], P(('dp', 'expert')), may hold values from 0 to 1, as said below
- w_gate: bfloat16 [8, 3072, 8192], P('expert', None, ('dp', 'cuts')), may hold values from -0.109375 to 0.109375
- w_up: bfloat16 [8, 3072, 8192], P('expert', None, ('dp', 'cuts')), may hold values from -0.109375 to 0.109375
- w_down: bfloat16 [8, 8192, 3072], P('expert', ('dp', 'cuts')), may hold values from -0.0625 to 0.0625
Outputs:
- token_grad: bfloat16 [4096, 3072], P(('dp', 'expert'), 'cuts')
- grad_gate: bfloat16 [8, 3072, 8192], P('expert', None, ('dp', 'cuts'))
- grad_up: bfloat16 [8, 3072, 8192], P('expert', None, ('dp', 'cuts'))
- grad_down: bfloat16 [8, 8192, 3072], P('expert', ('dp', 'cuts'))
The draws below stay inside these ranges and needn't reach their ends.
Inputs may be any that keep to these rules, and one draw needn't show every extreme that they name: `expert_ids`: each token names 2 different experts. `slot_ids`: within the 128 rows of one block, the choices are given slots in order of choice (all first choices before second ones) and then of row, counted for each expert; a choice whose count reaches 36 is dropped and has slot 0. In the rows of every index of dp, one expert is filled to 36 from every block. `keep_mask`: 1 exactly where the choice's count in its block is under 36.
All inputs are finite; a program needn't handle non-finite values.
Results may differ from the reference program's by a relative error of at most 0.0058.
Values may be sent and summed in bfloat16 or wider, within the bound.
No kernel may reach another device: no remote copies, remote signals or barrier semaphores. Data moves between devices by JAX's collectives and lax.ppermute only.
A program may use at most 128 MiB of HBM per device.

```python
import jax
import jax.numpy as jnp
from jax import lax

D = 3072
FF = 8192
TOPK = 2
TOK_DEV = 128
EXPERTS = 8
SOURCES = 32
CAP = 36
ROWS = 1152
TOKENS = 4096


def routing_tables(key):
    key = jax.random.fold_in(key, 11)
    blocks = TOKENS // TOK_DEV
    extra = CAP + CAP // 4 + 1
    subkeys = jax.random.split(key, 3)
    noise = jax.random.randint(subkeys[0], (blocks, TOK_DEV, EXPERTS), 0, 1000)
    hot_expert = jax.random.randint(subkeys[1], (blocks // EXPERTS,), 0, EXPERTS)
    hot_block = jnp.repeat(hot_expert, EXPERTS)
    ranks = jax.vmap(lambda single: jax.random.permutation(single, TOK_DEV))(jax.random.split(subkeys[2], blocks))
    forced = (ranks < extra).astype(jnp.int32)
    lift = forced[:, :, None] * (jnp.arange(EXPERTS)[None, None, :] == hot_block[:, None, None]).astype(jnp.int32)
    scores = (noise + 2000 * lift) * EXPERTS + jnp.arange(EXPERTS)[None, None, :]
    chosen = lax.top_k(scores, TOPK)[1].astype(jnp.int32)
    order = jnp.transpose(chosen, (0, 2, 1)).reshape(blocks, TOPK * TOK_DEV)
    onehot = (order[:, :, None] == jnp.arange(EXPERTS)[None, None, :]).astype(jnp.int32)
    before = jnp.cumsum(onehot, axis=1) - onehot
    place = jnp.sum(before * onehot, axis=2)
    kept = (place < CAP).astype(jnp.int32)
    place = place * kept
    return (unfold(order, blocks), unfold(place, blocks), unfold(kept, blocks))


def unfold(values, blocks):
    return jnp.transpose(values.reshape(blocks, TOPK, TOK_DEV), (0, 2, 1)).reshape(TOKENS, TOPK).astype(jnp.int32)


def draw_expert_ids(key, part):
    return routing_tables(key)[0]


def draw_slot_ids(key, part):
    return routing_tables(key)[1]


def draw_keep_mask(key, part):
    return routing_tables(key)[2]


def block_scale(rng, dims, cuts, smallest, top_value):
    loudness, own = 1.0, jax.random.fold_in(rng, 6)
    for position, parts in cuts:
        draws = jnp.exp(jax.random.uniform(jax.random.fold_in(own, position), (parts,), jnp.float32, smallest / len(cuts), top_value / len(cuts)))
        loudness = loudness * jnp.repeat(draws, dims[position] // parts).reshape([-1 if axis == position else 1 for axis in range(len(dims))])
    return loudness


def scatter_about(key, dims, spread, most, shards=(), kind=jnp.bfloat16):
    values = spread * jax.random.normal(key, dims, jnp.float32)
    if shards:
        values = values * block_scale(key, dims, shards, -0.22, 0.18)
    return jnp.clip(values, -most, most).astype(kind)


def setup_inputs(seed: int = 0) -> dict:
    seeds = jax.random.split(jax.random.key(seed), 10)
    return {
        "tokens": scatter_about(seeds[0], (TOKENS, D), 1.0, 6.0, ((0, 32), (1, 8))),
        "cotangent": scatter_about(seeds[1], (TOKENS, D), 1.0, 6.0, ((0, 32), (1, 8))),
        "combine": jnp.clip(0.25 + 0.75 * jax.random.uniform(seeds[2], (TOKENS, TOPK), jnp.float32) ** block_scale(seeds[2], (TOKENS, TOPK), ((0, 32),), -0.2, 0.2), 0.25, 1.0),
        "expert_ids": draw_expert_ids(jax.random.fold_in(seeds[9], 71), 0),
        "slot_ids": draw_slot_ids(jax.random.fold_in(seeds[9], 71), 0),
        "keep_mask": draw_keep_mask(jax.random.fold_in(seeds[9], 71), 0),
        "w_gate": scatter_about(seeds[6], (EXPERTS, D, FF), D ** -0.5, 0.109375, ((0, 8), (2, 32))),
        "w_up": scatter_about(seeds[7], (EXPERTS, D, FF), D ** -0.5, 0.109375, ((0, 8), (2, 32))),
        "w_down": scatter_about(seeds[8], (EXPERTS, FF, D), FF ** -0.5, 0.0625, ((0, 8), (1, 32))),
    }


def expert_pass(expert_rows, scaled_rows, gate_weight_block, up_weight_block, down_weight_block):
    gate_pre = jnp.dot(expert_rows, gate_weight_block, preferred_element_type=jnp.float32)
    up_pre = jnp.dot(expert_rows, up_weight_block, preferred_element_type=jnp.float32)
    squash = jax.nn.sigmoid(gate_pre)
    active = gate_pre * squash
    hidden_state = (active * up_pre).astype(jnp.bfloat16)
    hidden_grad = jnp.dot(scaled_rows, down_weight_block.T, preferred_element_type=jnp.float32)
    gate_gradient = (hidden_grad * up_pre * (squash * (1.0 + gate_pre * (1.0 - squash)))).astype(jnp.bfloat16)
    up_gradient = (hidden_grad * active).astype(jnp.bfloat16)
    grad_gate = jnp.dot(expert_rows.T, gate_gradient, preferred_element_type=jnp.float32).astype(jnp.bfloat16)
    grad_up = jnp.dot(expert_rows.T, up_gradient, preferred_element_type=jnp.float32).astype(jnp.bfloat16)
    grad_down = jnp.dot(hidden_state.T, scaled_rows, preferred_element_type=jnp.float32).astype(jnp.bfloat16)
    row_grads = jnp.dot(gate_gradient, gate_weight_block.T, preferred_element_type=jnp.float32) + jnp.dot(up_gradient, up_weight_block.T, preferred_element_type=jnp.float32)
    return grad_gate, grad_up, grad_down, row_grads


def reference(tokens, cotangent, combine, expert_ids, slot_ids, keep_mask, w_gate, w_up, w_down):
    block_index = jnp.arange(TOKENS, dtype=jnp.int32) // TOK_DEV
    target = ((expert_ids * SOURCES + block_index[:, None]) * CAP + slot_ids).astype(jnp.int32)
    spare_row = EXPERTS * ROWS
    landing = jnp.where(keep_mask > 0, target, spare_row).reshape(-1)
    copies = jnp.broadcast_to(tokens[:, None, :], (TOKENS, TOPK, D)).reshape(-1, D)
    scaled = (combine[:, :, None] * cotangent.astype(jnp.float32)[:, None, :]).astype(jnp.bfloat16).reshape(-1, D)
    expert_rows = jnp.zeros((spare_row + 1, D), jnp.bfloat16).at[landing].set(copies)[:spare_row].reshape(EXPERTS, ROWS, D)
    scaled_rows = jnp.zeros((spare_row + 1, D), jnp.bfloat16).at[landing].set(scaled)[:spare_row].reshape(EXPERTS, ROWS, D)
    grad_gate, grad_up, grad_down, row_grads = lax.map(lambda items: expert_pass(*items), (expert_rows, scaled_rows, w_gate, w_up, w_down))
    flat_rows = row_grads.reshape(spare_row, D)
    token_grad = jnp.zeros((TOKENS, D), jnp.float32)
    for index in range(TOPK):
        picked = flat_rows[target[:, index]]
        token_grad = token_grad + jnp.where(keep_mask[:, index:index + 1] > 0, picked, 0.0)
    return token_grad.astype(jnp.bfloat16), grad_gate, grad_up, grad_down
```

```python
import jax
import jax.numpy as jnp
from jax import lax
from jax.experimental import pallas as pl
from jax.experimental.pallas import tpu as pltpu
from jax.sharding import Mesh, PartitionSpec as P

TOPK = 2
BF = jnp.bfloat16
F32 = jnp.float32


def shift(size, step):
    return [(i, (i + step) % size) for i in range(size)]


def zshift(flip, step):
    return [(h * 4 + l, (h ^ flip) * 4 + (l + step) % 4) for h in range(2) for l in range(4)]


def up_kernel(rows_ref, gate_ref, up_ref, down_ref, grads_ref, hidden_ref):
    cuts, _, width = rows_ref.shape[1:]
    cut = width // 2
    gate = up = back = None
    for v in range(cuts):
        part = pl.ds(v * cut, cut)
        token_rows = rows_ref[0, v, :, :cut]
        scaled_rows = rows_ref[0, v, :, cut:]
        g = jnp.dot(token_rows, gate_ref[part, :], preferred_element_type=F32)
        u = jnp.dot(token_rows, up_ref[part, :], preferred_element_type=F32)
        h = lax.dot_general(
            scaled_rows,
            down_ref[:, part],
            (((1,), (1,)), ((), ())),
            preferred_element_type=F32,
        )
        gate = g if gate is None else gate + g
        up = u if up is None else up + u
        back = h if back is None else back + h
    squash = jax.nn.sigmoid(gate)
    active = gate * squash
    units = gate.shape[1]
    hidden_ref[0] = (active * up).astype(BF)
    grads_ref[0, :, :units] = (back * up * (squash * (1.0 + gate * (1.0 - squash)))).astype(BF)
    grads_ref[0, :, units:] = (back * active).astype(BF)


def up_pass(collected, gate_w, up_w, down_w):
    blocks, cuts, rows, width = collected.shape
    model, units = gate_w.shape
    return pl.pallas_call(
        up_kernel,
        grid=(blocks,),
        in_specs=[
            pl.BlockSpec((1, cuts, rows, width), lambda i: (i, 0, 0, 0)),
            pl.BlockSpec((model, units), lambda i: (0, 0)),
            pl.BlockSpec((model, units), lambda i: (0, 0)),
            pl.BlockSpec((units, model), lambda i: (0, 0)),
        ],
        out_specs=[
            pl.BlockSpec((1, rows, 2 * units), lambda i: (i, 0, 0)),
            pl.BlockSpec((1, rows, units), lambda i: (i, 0, 0)),
        ],
        out_shape=[
            jax.ShapeDtypeStruct((blocks, rows, 2 * units), BF),
            jax.ShapeDtypeStruct((blocks, rows, units), BF),
        ],
        compiler_params=pltpu.CompilerParams(vmem_limit_bytes=48 * 1024 * 1024),
        cost_estimate=pl.CostEstimate(
            flops=6 * blocks * rows * model * units,
            bytes_accessed=2 * blocks * rows * 2 * model,
            transcendentals=blocks * rows * units,
        ),
    )(collected, gate_w, up_w, down_w)


def shards(tokens, cotangent, combine, expert_ids, slot_ids, keep_mask, w_gate, w_up, w_down):
    experts = 8
    tok_rows, cut = tokens.shape
    capacity = 9 * tok_rows * TOPK // (8 * experts)
    slots = experts * capacity
    zh, zl = lax.axis_index("zh"), lax.axis_index("zl")
    y, c = lax.axis_index("y"), lax.axis_index("c")
    kept = keep_mask > 0

    place = jnp.where(kept, (expert_ids // 2) * (2 * capacity) + slot_ids, -1)
    mine = jnp.where((expert_ids % 2) == zh, place, -1)
    theirs = jnp.where((expert_ids % 2) != zh, place, -1)
    theirs = lax.ppermute(theirs, "zh", [(0, 1), (1, 0)])

    target = jnp.where(kept, expert_ids * capacity + slot_ids, -1)
    positions = jnp.arange(slots, dtype=jnp.int32)[:, None]
    routes = [positions == target[:, k][None, :] for k in range(TOPK)]
    pick = (routes[0] | routes[1]).astype(BF)
    weight = sum(
        jnp.sum(jnp.where(routes[k], combine[:, k][None, :], 0.0), axis=1, keepdims=True)
        for k in range(TOPK)
    )
    both = jnp.dot(pick, jnp.concatenate([tokens, cotangent], axis=1), preferred_element_type=F32)
    sent = jnp.concatenate(
        [both[:, :cut].astype(BF), (both[:, cut:] * weight).astype(BF)], axis=1
    )
    received = lax.all_to_all(
        sent.reshape(experts, capacity, 2 * cut), ("x", "zh"), split_axis=0, concat_axis=0, tiled=True
    )
    collected = lax.all_gather(
        received.reshape(1, slots, 2 * cut), ("y", "zl", "c"), axis=0, tiled=True
    ).reshape(4, 8, slots, 2 * cut)

    gate_w, up_w, down_w = w_gate[0], w_up[0], w_down[0]
    grads, hidden = up_pass(collected, gate_w, up_w, down_w)
    units = gate_w.shape[1]

    def turned(owner):
        joined = jnp.concatenate([gate_w, up_w], axis=1).reshape(4, 2, cut, 2 * units)
        joined = jnp.concatenate([joined, joined[:3]], axis=0)
        return lax.dynamic_slice(joined, (zl, owner, 0, 0), (4, 1, cut, 2 * units)).reshape(
            4 * cut, 2 * units
        )

    near, far = turned(c), turned(1 - c)
    half = 2 * cut
    swap = [(0, 1), (1, 0)]

    def block(step):
        return lax.dynamic_index_in_dim(grads, (y + step) % 4, 0, keepdims=False)

    def product(rows, weights):
        return lax.dot_general(rows, weights, (((1,), (1,)), ((), ())), preferred_element_type=F32)

    def halves(step):
        rows = block(step)
        got = lax.ppermute(product(rows, far).astype(BF), "c", swap).astype(F32)
        return (
            product(rows, near[:half]) + got[:, :half],
            product(rows, near[half:]) + got[:, half:],
        )

    up_y = lambda v: lax.ppermute(v.astype(BF), "y", shift(4, 1)).astype(F32)
    down_y = lambda v: lax.ppermute(v.astype(BF), "y", shift(4, -1)).astype(F32)
    across = halves(2)
    relay_a = up_y(across[0])
    relay_b = down_y(across[1])
    above, below = halves(1), halves(3)
    from_below_b = up_y(above[1])
    from_above_a = down_y(below[0])
    from_below_a = up_y(above[0] + relay_a)
    from_above_b = down_y(below[1] + relay_b)
    own = halves(0)
    rows = jnp.concatenate(
        [own[0] + from_below_a + from_above_a, own[1] + from_below_b + from_above_b], axis=1
    ).astype(BF)

    x = lax.axis_index("x")
    rows = rows.reshape(4, 2 * capacity, 4 * cut)
    returned = [lax.dynamic_index_in_dim(rows, x, 0, keepdims=False)]
    for step in (1, 3, 2):
        piece = lax.dynamic_index_in_dim(rows, (x + step) % 4, 0, keepdims=False)
        returned.append(lax.ppermute(piece, "x", shift(4, step)))
    returned = jnp.concatenate([returned[0], returned[1], returned[3], returned[2]], axis=0)

    slot_base = jnp.arange(slots, dtype=jnp.int32)[None, :]
    def spread(places, owner_zh):
        owner = places // (2 * capacity)
        slot = places % (2 * capacity)
        column = ((x - owner) % 4) * (2 * capacity) + owner_zh * capacity + slot
        column = jnp.where(places >= 0, column, -1)
        return ((slot_base == column[:, 0:1]) | (slot_base == column[:, 1:2])).astype(BF)

    routes_back = jnp.concatenate([spread(mine, zh), spread(theirs, 1 - zh)], axis=0)
    parts = jnp.dot(routes_back, returned, preferred_element_type=F32).astype(BF)
    parts = parts.reshape(2, tok_rows, 4, cut)
    total = parts[0, :, 0].astype(F32)
    for flip in range(2):
        for step in range(4):
            if flip == 0 and step == 0:
                continue
            got = lax.ppermute(parts[flip, :, step], ("zh", "zl"), zshift(flip, step))
            total = total + got.astype(F32)
    token_grad = total.astype(BF)

    grads_all = grads.reshape(4, slots, 2 * units)
    token_part = collected[..., :cut]
    scaled_part = collected[..., cut:]
    grad_gate = jnp.einsum(
        "hiyb,hys->ibs", token_part, grads_all[..., :units], preferred_element_type=F32
    )
    grad_up = jnp.einsum(
        "hiyb,hys->ibs", token_part, grads_all[..., units:], preferred_element_type=F32
    )
    grad_down = jnp.einsum("hpt,hmpu->tmu", hidden, scaled_part, preferred_element_type=F32)
    return (
        token_grad,
        grad_gate.astype(BF).reshape(1, experts * cut, -1),
        grad_up.astype(BF).reshape(1, experts * cut, -1),
        grad_down.astype(BF).reshape(1, -1, experts * cut),
    )


def solution(mesh):
    fine = Mesh(mesh.devices.reshape(4, 4, 2, 4, 2), ("y", "x", "zh", "zl", "c"))
    tok = ("y", "x", "zh")
    cuts = ("zl", "c")
    hid = ("y", "zl", "c")
    return jax.shard_map(
        shards,
        mesh=fine,
        in_specs=(
            P(tok, cuts),
            P(tok, cuts),
            P(tok, None),
            P(tok, None),
            P(tok, None),
            P(tok, None),
            P(("x", "zh"), None, hid),
            P(("x", "zh"), None, hid),
            P(("x", "zh"), hid, None),
        ),
        out_specs=(
            P(tok, cuts),
            P(("x", "zh"), None, hid),
            P(("x", "zh"), None, hid),
            P(("x", "zh"), hid, None),
        ),
        check_vma=False,
    )
```

```python
import jax
import jax.numpy as jnp
from jax import lax
from jax.experimental import pallas as pl
from jax.experimental.pallas import tpu as pltpu
from jax.sharding import Mesh, PartitionSpec as P

TOPK = 2
BF = jnp.bfloat16
F32 = jnp.float32
SWAP = [(0, 1), (1, 0)]


def ring(step):
    return [(i, (i + step) % 4) for i in range(4)]


def zshift(flip, step):
    return [(h * 4 + l, (h ^ flip) * 4 + (l + step) % 4) for h in range(2) for l in range(4)]


def over_x(value, step):
    return lax.ppermute(value, "x", ring(step))


def over_y(value, step):
    return lax.ppermute(value, "y", ring(step))


def over_zl(value, step):
    return lax.ppermute(value, "zl", ring(step))


def over_z(value, flip, step):
    return lax.ppermute(value, ("zh", "zl"), zshift(flip, step))


def over_core(value):
    return lax.ppermute(value, "c", SWAP)


def dot(a, b):
    return jnp.dot(a, b, preferred_element_type=F32)


def dot_nt(a, b):
    return lax.dot_general(a, b, (((1,), (1,)), ((), ())), preferred_element_type=F32)


def dot_tn(a, b):
    return lax.dot_general(a, b, (((0,), (0,)), ((), ())), preferred_element_type=F32)


def rows_kernel(info_ref, *refs):
    near, far, grads = refs[:4], refs[4:8], refs[8:12]
    gate_ref, up_ref = refs[12:]
    cut = near[0].shape[1]
    units = gate_ref.shape[1]
    first = info_ref[1] == 0
    a = sum(dot_tn(near[r][...], grads[r][...]) for r in range(4))
    b = sum(dot_tn(far[r][...], grads[r][...]) for r in range(4))
    low = jnp.where(first, a, b).astype(BF)
    high = jnp.where(first, b, a).astype(BF)
    gate_ref[:cut, :] = low[:, :units]
    gate_ref[cut:, :] = high[:, :units]
    up_ref[:cut, :] = low[:, units:]
    up_ref[cut:, :] = high[:, units:]


def down_kernel(info_ref, *refs):
    near, far, hidden = refs[:4], refs[4:8], refs[8:12]
    down_ref = refs[12]
    cut = near[0].shape[1]
    first = info_ref[1] == 0
    a = sum(dot_tn(hidden[r][...], near[r][...]) for r in range(4))
    b = sum(dot_tn(hidden[r][...], far[r][...]) for r in range(4))
    down_ref[:, :cut] = jnp.where(first, a, b).astype(BF)
    down_ref[:, cut:] = jnp.where(first, b, a).astype(BF)


def weight_pass(kernel, info, near, far, factors, outs, by_rows):
    rows, columns = near[0].shape
    cut = columns // 4

    def turned(j, info_ref):
        place = (info_ref[0] + j) % 4
        return (place, 0) if by_rows else (0, place)

    row_specs = [pl.BlockSpec((rows, cut), lambda j, info_ref: (0, j))] * 8
    factor_specs = [pl.BlockSpec(f.shape, lambda j, info_ref: (0, 0)) for f in factors]
    blocks = [(s[0] // 4, s[1]) if by_rows else (s[0], s[1] // 4) for s in outs]
    width = factors[0].shape[1]
    return pl.pallas_call(
        kernel,
        grid_spec=pltpu.PrefetchScalarGridSpec(
            num_scalar_prefetch=1,
            grid=(4,),
            in_specs=row_specs + factor_specs,
            out_specs=[pl.BlockSpec(b, turned) for b in blocks],
        ),
        out_shape=[jax.ShapeDtypeStruct(s, BF) for s in outs],
        compiler_params=pltpu.CompilerParams(vmem_limit_bytes=32 * 1024 * 1024),
        cost_estimate=pl.CostEstimate(
            flops=2 * 4 * rows * 8 * cut * width, bytes_accessed=2 * 4 * rows * 8 * cut, transcendentals=0
        ),
    )(info, *near, *far, *factors)


def shards(tokens, cotangent, combine, expert_ids, slot_ids, keep_mask, w_gate, w_up, w_down):
    experts = 8
    tok_rows, cut = tokens.shape
    capacity = 9 * tok_rows * TOPK // (8 * experts)
    pair = 2 * capacity
    slots = experts * capacity
    units = w_gate.shape[2]
    half = 2 * cut
    x, zh = lax.axis_index("x"), lax.axis_index("zh")
    zl, c = lax.axis_index("zl"), lax.axis_index("c")
    info = jnp.stack([zl, c]).astype(jnp.int32)

    kept = keep_mask > 0
    target = jnp.where(kept, expert_ids * capacity + slot_ids, -1)
    positions = jnp.arange(slots, dtype=jnp.int32)
    routes = [positions[:, None] == target[:, k][None, :] for k in range(TOPK)]
    pick = (routes[0] | routes[1]).astype(BF)
    weight = sum(
        jnp.sum(jnp.where(routes[k], combine[:, k][None, :], 0.0), axis=1, keepdims=True)
        for k in range(TOPK)
    )
    both = dot(pick, jnp.concatenate([tokens, cotangent], axis=1))
    sent = jnp.concatenate(
        [both[:, :cut].astype(BF), (both[:, cut:] * weight).astype(BF)], axis=1
    )
    received = lax.all_to_all(
        sent.reshape(experts, capacity, 2 * cut), ("x", "zh"), split_axis=0, concat_axis=0, tiled=True
    ).reshape(slots, 2 * cut)
    token_rows, scaled_rows = received[:, :cut], received[:, cut:]

    def turn_z(rows):
        return [rows] + [over_zl(rows, -j) for j in range(1, 4)]

    def from_sides(own):
        return over_y(own, -1), over_y(own, 1)

    def relayed(above, below):
        return over_y(below[:, :half], 1), over_y(above[:, half:], -1)

    pieces = turn_z(token_rows)
    w_gate, w_up, w_down, pieces[1] = lax.optimization_barrier((w_gate, w_up, w_down, pieces[1]))
    token_own = jnp.concatenate(pieces, axis=1)
    token_own, scaled_rows = lax.optimization_barrier((token_own, scaled_rows))
    scaled_own = jnp.concatenate(turn_z(scaled_rows), axis=1)
    expert_ids, keep_mask, scaled_own = lax.optimization_barrier((expert_ids, keep_mask, scaled_own))

    kept = keep_mask > 0
    place = jnp.where(kept, (expert_ids // 2) * pair + slot_ids, -1)
    mine = jnp.where((expert_ids % 2) == zh, place, -1)
    theirs = jnp.where((expert_ids % 2) != zh, place, -1)
    theirs = lax.ppermute(theirs, "zh", SWAP)

    def spread(places, block):
        column = ((places // pair - x) % 4) * pair + block * capacity + places % pair
        column = jnp.where(places >= 0, column, -1)
        return (
            (positions[None, :] == column[:, 0:1]) | (positions[None, :] == column[:, 1:2])
        ).astype(BF)

    back = jnp.concatenate([spread(mine, zh), spread(theirs, 1 - zh)], axis=0)

    joined = jnp.concatenate([w_gate[0], w_up[0]], axis=1).reshape(4, 2, cut, 2 * units)
    joined = jnp.concatenate([joined, joined[:3]], axis=0)

    down = w_down[0].reshape(units, 4, 2, cut)
    down = jnp.concatenate([down, down[:, :3]], axis=1)

    def turned(owner):
        rows = lax.dynamic_slice(joined, (zl, owner, 0, 0), (4, 1, cut, 2 * units))
        cols = lax.dynamic_slice(down, (0, zl, owner, 0), (units, 4, 1, cut))
        return rows.reshape(4 * cut, 2 * units), cols.reshape(units, 4 * cut)

    (near_w, near_down), (far_w, far_down) = turned(c), turned(1 - c)

    token_above, token_below = from_sides(token_own)
    token_across = jnp.concatenate(relayed(token_above, token_below), axis=1)
    token_near = [token_across, token_above, token_below, token_own]
    token_far = [over_core(v) for v in token_near]
    scaled_above, scaled_below = from_sides(scaled_own)
    scaled_across = relayed(scaled_above, scaled_below)
    scaled_near = [None, scaled_above, scaled_below, scaled_own]
    scaled_far = [None] + [over_core(v) for v in scaled_near[1:]]
    grads, hidden = [None] * 4, [None] * 4

    def unit_pass(r):
        pre = dot(token_near[r], near_w) + dot(token_far[r], far_w)
        back_pre = dot_nt(scaled_near[r], near_down) + dot_nt(scaled_far[r], far_down)
        gate, up = pre[:, :units], pre[:, units:]
        squash = jax.nn.sigmoid(gate)
        active = gate * squash
        hidden[r] = (active * up).astype(BF)
        gate_grad = (back_pre * up * (squash * (1.0 + gate * (1.0 - squash)))).astype(BF)
        up_grad = (back_pre * active).astype(BF)
        grads[r] = jnp.concatenate([gate_grad, up_grad], axis=1)

    model = experts * cut

    def halves(r):
        got = over_core(dot_nt(grads[r], far_w).astype(BF)).astype(F32)
        return (
            dot_nt(grads[r], near_w[:half]) + got[:, :half],
            dot_nt(grads[r], near_w[half:]) + got[:, half:],
        )

    unit_pass(1)
    unit_pass(2)
    above, below = halves(1), halves(2)
    above_b, below_a = above[1].astype(BF), below[0].astype(BF)
    from_below_b = over_y(above_b, 1)
    from_above_a = over_y(below_a, -1)
    scaled_across, above_b, below_a = lax.optimization_barrier((scaled_across, above_b, below_a))
    scaled_near[0] = jnp.concatenate(scaled_across, axis=1)
    scaled_far[0] = over_core(scaled_near[0])
    unit_pass(0)
    unit_pass(3)
    across = halves(0)
    across_a, across_b = across[0].astype(BF), across[1].astype(BF)
    relay_a = over_y(across_a, 1)
    relay_b = over_y(across_b, -1)
    later, across_a, across_b = lax.optimization_barrier((grads, across_a, across_b))
    grad_gate, grad_up = weight_pass(
        rows_kernel, info, token_near, token_far, later, [(model, units), (model, units)], True
    )
    relay_a, relay_b, grad_gate, grad_up = lax.optimization_barrier(
        (relay_a, relay_b, grad_gate, grad_up)
    )
    from_below_a = over_y((above[0] + relay_a.astype(F32)).astype(BF), 1)
    from_above_b = over_y((below[1] + relay_b.astype(F32)).astype(BF), -1)
    own = halves(3)
    (grad_down,) = weight_pass(
        down_kernel, info, scaled_near, scaled_far, hidden, [(units, model)], False
    )
    from_below_a, from_above_b, grad_down = lax.optimization_barrier(
        (from_below_a, from_above_b, grad_down)
    )
    rows = jnp.concatenate(
        [
            own[0] + from_below_a.astype(F32) + from_above_a.astype(F32),
            own[1] + from_below_b.astype(F32) + from_above_b.astype(F32),
        ],
        axis=1,
    ).astype(BF)

    rows = rows.reshape(4, pair, 4 * cut)
    pieces = [lax.dynamic_index_in_dim(rows, x, 0, keepdims=False)]
    for s in range(1, 4):
        piece = lax.dynamic_index_in_dim(rows, (x + 4 - s) % 4, 0, keepdims=False)
        pieces.append(over_x(piece, -s))
    sums = dot(back, jnp.concatenate(pieces, axis=0)).astype(BF)
    total = sums[:tok_rows, :cut].astype(F32)
    for flip in range(2):
        for j in range(4):
            if flip or j:
                piece = sums[flip * tok_rows : (flip + 1) * tok_rows, j * cut : (j + 1) * cut]
                total = total + over_z(piece, flip, j).astype(F32)
    return total.astype(BF), grad_gate[None], grad_up[None], grad_down[None]


def solution(mesh):
    fine = Mesh(mesh.devices.reshape(4, 4, 2, 4, 2), ("y", "x", "zh", "zl", "c"))
    tok = ("y", "x", "zh")
    cuts = ("zl", "c")
    hid = ("y", "zl", "c")
    return jax.shard_map(
        shards,
        mesh=fine,
        in_specs=(
            P(tok, cuts),
            P(tok, cuts),
            P(tok, None),
            P(tok, None),
            P(tok, None),
            P(tok, None),
            P(("x", "zh"), None, hid),
            P(("x", "zh"), None, hid),
            P(("x", "zh"), hid, None),
        ),
        out_specs=(
            P(tok, cuts),
            P(("x", "zh"), None, hid),
            P(("x", "zh"), None, hid),
            P(("x", "zh"), hid, None),
        ),
        check_vma=False,
    )
```

```python
import jax
import jax.numpy as jnp
from jax import lax
from jax.experimental import pallas as pl
from jax.experimental.pallas import tpu as pltpu
from jax.sharding import Mesh, PartitionSpec as P

TOPK = 2
BF = jnp.bfloat16
F32 = jnp.float32
SWAP = [(0, 1), (1, 0)]


def ring(step):
    return [(i, (i + step) % 4) for i in range(4)]


def zshift(flip, step):
    return [(h * 4 + l, (h ^ flip) * 4 + (l + step) % 4) for h in range(2) for l in range(4)]


def over_x(value, step):
    return lax.ppermute(value, "x", ring(step))


def over_y(value, step):
    return lax.ppermute(value, "y", ring(step))


def over_zl(value, step):
    return lax.ppermute(value, "zl", ring(step))


def over_z(value, flip, step):
    return lax.ppermute(value, ("zh", "zl"), zshift(flip, step))


def over_core(value):
    return lax.ppermute(value, "c", SWAP)


def dot(a, b):
    return jnp.dot(a, b, preferred_element_type=F32)


def dot_nt(a, b):
    return lax.dot_general(a, b, (((1,), (1,)), ((), ())), preferred_element_type=F32)


def dot_tn(a, b):
    return lax.dot_general(a, b, (((0,), (0,)), ((), ())), preferred_element_type=F32)


def rows_kernel(info_ref, *refs):
    near, far, grads = refs[:4], refs[4:8], refs[8:12]
    gate_ref, up_ref = refs[12:]
    cut = near[0].shape[1]
    units = gate_ref.shape[1]
    first = info_ref[1] == 0
    a = sum(dot_tn(near[r][...], grads[r][...]) for r in range(4))
    b = sum(dot_tn(far[r][...], grads[r][...]) for r in range(4))
    low = jnp.where(first, a, b).astype(BF)
    high = jnp.where(first, b, a).astype(BF)
    gate_ref[:cut, :] = low[:, :units]
    gate_ref[cut:, :] = high[:, :units]
    up_ref[:cut, :] = low[:, units:]
    up_ref[cut:, :] = high[:, units:]


def down_kernel(info_ref, *refs):
    near, far, hidden = refs[:4], refs[4:8], refs[8:12]
    down_ref = refs[12]
    cut = near[0].shape[1]
    first = info_ref[1] == 0
    a = sum(dot_tn(hidden[r][...], near[r][...]) for r in range(4))
    b = sum(dot_tn(hidden[r][...], far[r][...]) for r in range(4))
    down_ref[:, :cut] = jnp.where(first, a, b).astype(BF)
    down_ref[:, cut:] = jnp.where(first, b, a).astype(BF)


def weight_pass(kernel, info, near, far, factors, outs, by_rows):
    rows, columns = near[0].shape
    cut = columns // 4

    def turned(j, info_ref):
        place = (info_ref[0] + j) % 4
        return (place, 0) if by_rows else (0, place)

    row_specs = [pl.BlockSpec((rows, cut), lambda j, info_ref: (0, j))] * 8
    factor_specs = [pl.BlockSpec(f.shape, lambda j, info_ref: (0, 0)) for f in factors]
    blocks = [(s[0] // 4, s[1]) if by_rows else (s[0], s[1] // 4) for s in outs]
    width = factors[0].shape[1]
    return pl.pallas_call(
        kernel,
        grid_spec=pltpu.PrefetchScalarGridSpec(
            num_scalar_prefetch=1,
            grid=(4,),
            in_specs=row_specs + factor_specs,
            out_specs=[pl.BlockSpec(b, turned) for b in blocks],
        ),
        out_shape=[jax.ShapeDtypeStruct(s, BF) for s in outs],
        compiler_params=pltpu.CompilerParams(vmem_limit_bytes=32 * 1024 * 1024),
        cost_estimate=pl.CostEstimate(
            flops=2 * 4 * rows * 8 * cut * width, bytes_accessed=2 * 4 * rows * 8 * cut, transcendentals=0
        ),
    )(info, *near, *far, *factors)


def shards(tokens, cotangent, combine, expert_ids, slot_ids, keep_mask, w_gate, w_up, w_down):
    experts = 8
    tok_rows, cut = tokens.shape
    capacity = 9 * tok_rows * TOPK // (8 * experts)
    pair = 2 * capacity
    slots = experts * capacity
    units = w_gate.shape[2]
    half = 2 * cut
    x, zh = lax.axis_index("x"), lax.axis_index("zh")
    zl, c = lax.axis_index("zl"), lax.axis_index("c")
    info = jnp.stack([zl, c]).astype(jnp.int32)

    kept = keep_mask > 0
    target = ((expert_ids // 2 - x) % 4) * pair + (expert_ids % 2 != zh) * capacity + slot_ids
    target = jnp.where(kept, target, -1)
    positions = jnp.arange(slots, dtype=jnp.int32)
    routes = [positions[:, None] == target[:, k][None, :] for k in range(TOPK)]
    pick = (routes[0] | routes[1]).astype(BF)
    weight = sum(
        jnp.sum(jnp.where(routes[k], combine[:, k][None, :], 0.0), axis=1, keepdims=True)
        for k in range(TOPK)
    )
    both = dot(pick, jnp.concatenate([tokens, cotangent], axis=1))
    sent = jnp.concatenate([both[:, :cut], both[:, cut:] * weight], axis=1).astype(BF)
    got = [sent[:pair]] + [over_x(sent[s * pair : (s + 1) * pair], s) for s in range(1, 4)]
    got = jnp.stack(got).reshape(4, 2, capacity, 2 * cut)

    sides = [got[:, flip].reshape(slots // 2, 2 * cut) for flip in range(2)]
    own_rows = jnp.concatenate([sides[0], lax.ppermute(sides[1], "zh", SWAP)], axis=0)
    token_rows, scaled_rows = own_rows[:, :cut], own_rows[:, cut:]

    def turn_z(rows):
        return [rows] + [over_zl(rows, -j) for j in range(1, 4)]

    def from_sides(own):
        return over_y(own, -1), over_y(own, 1)

    def relayed(above, below):
        return over_y(below[:, :half], 1), over_y(above[:, half:], -1)

    pieces = turn_z(token_rows)
    w_gate, w_up, w_down, pieces[1] = lax.optimization_barrier((w_gate, w_up, w_down, pieces[1]))
    token_own = jnp.concatenate(pieces, axis=1)
    token_own, scaled_rows = lax.optimization_barrier((token_own, scaled_rows))
    scaled_own = jnp.concatenate(turn_z(scaled_rows), axis=1)

    joined = jnp.concatenate([w_gate[0], w_up[0]], axis=1).reshape(4, 2, cut, 2 * units)
    joined = jnp.concatenate([joined, joined[:3]], axis=0)

    down = w_down[0].reshape(units, 4, 2, cut)
    down = jnp.concatenate([down, down[:, :3]], axis=1)

    def turned(owner):
        rows = lax.dynamic_slice(joined, (zl, owner, 0, 0), (4, 1, cut, 2 * units))
        cols = lax.dynamic_slice(down, (0, zl, owner, 0), (units, 4, 1, cut))
        return rows.reshape(4 * cut, 2 * units), cols.reshape(units, 4 * cut)

    (near_w, near_down), (far_w, far_down) = turned(c), turned(1 - c)

    token_above, token_below = from_sides(token_own)
    token_across = relayed(token_above, token_below)
    scaled_above, scaled_below = from_sides(scaled_own)
    token_across, scaled_above, scaled_below = lax.optimization_barrier(
        (token_across, scaled_above, scaled_below)
    )
    scaled_across = relayed(scaled_above, scaled_below)
    token_near = [jnp.concatenate(token_across, axis=1), token_above, token_below, token_own]
    token_far = [over_core(v) for v in token_near]
    scaled_near = [None, scaled_above, scaled_below, scaled_own]
    scaled_far = [None] + [over_core(v) for v in scaled_near[1:]]
    grads, hidden = [None] * 4, [None] * 4

    def unit_pass(r):
        pre = dot(token_near[r], near_w) + dot(token_far[r], far_w)
        back_pre = dot_nt(scaled_near[r], near_down) + dot_nt(scaled_far[r], far_down)
        gate, up = pre[:, :units], pre[:, units:]
        squash = jax.nn.sigmoid(gate)
        active = gate * squash
        hidden[r] = (active * up).astype(BF)
        gate_grad = (back_pre * up * (squash * (1.0 + gate * (1.0 - squash)))).astype(BF)
        up_grad = (back_pre * active).astype(BF)
        grads[r] = jnp.concatenate([gate_grad, up_grad], axis=1)

    model = experts * cut

    def far_half(r):
        return dot_nt(grads[r], far_w).astype(BF)

    def halves(r, far_rows):
        got = over_core(far_rows).astype(F32)
        return (
            dot_nt(grads[r], near_w[:half]) + got[:, :half],
            dot_nt(grads[r], near_w[half:]) + got[:, half:],
        )

    unit_pass(1)
    unit_pass(2)
    far_above, far_below = far_half(1), far_half(2)
    scaled_across, far_above, far_below = lax.optimization_barrier((scaled_across, far_above, far_below))
    above, below = halves(1, far_above), halves(2, far_below)
    above_b, below_a = above[1].astype(BF), below[0].astype(BF)
    from_below_b = over_y(above_b, 1)
    from_above_a = over_y(below_a, -1)
    scaled_near[0] = jnp.concatenate(scaled_across, axis=1)
    scaled_far[0] = over_core(scaled_near[0])
    unit_pass(0)
    unit_pass(3)
    across = halves(0, far_half(0))
    across_a, across_b = across[0].astype(BF), across[1].astype(BF)
    relay_a = over_y(across_a, 1)
    relay_b = over_y(across_b, -1)
    later, across_a, across_b = lax.optimization_barrier((grads, across_a, across_b))
    grad_gate, grad_up = weight_pass(
        rows_kernel, info, token_near, token_far, later, [(model, units), (model, units)], True
    )
    relay_a, relay_b, grad_gate, grad_up = lax.optimization_barrier(
        (relay_a, relay_b, grad_gate, grad_up)
    )
    from_below_a = over_y((above[0] + relay_a.astype(F32)).astype(BF), 1)
    from_above_b = over_y((below[1] + relay_b.astype(F32)).astype(BF), -1)
    own = halves(3, far_half(3))
    (grad_down,) = weight_pass(
        down_kernel, info, scaled_near, scaled_far, hidden, [(units, model)], False
    )
    from_below_a, from_above_b, grad_down = lax.optimization_barrier(
        (from_below_a, from_above_b, grad_down)
    )
    rows = jnp.concatenate(
        [
            own[0] + from_below_a.astype(F32) + from_above_a.astype(F32),
            own[1] + from_below_b.astype(F32) + from_above_b.astype(F32),
        ],
        axis=1,
    ).astype(BF)

    sums = []
    for flip in range(2):
        total = None
        for j in range(4):
            piece = rows[flip * slots // 2 : (flip + 1) * slots // 2, j * cut : (j + 1) * cut]
            if flip or j:
                piece = over_z(piece, flip, j)
            total = piece.astype(F32) if total is None else total + piece.astype(F32)
        sums.append(total.astype(BF))
    place = positions // pair * capacity + positions % pair // capacity * (slots // 2) + positions % capacity
    order = (place[:, None] == positions[None, :]).astype(BF)
    sums = dot(order, jnp.concatenate(sums, axis=0)).astype(BF)
    returned = [sums[:pair]] + [over_x(sums[s * pair : (s + 1) * pair], -s) for s in range(1, 4)]
    total = dot_tn(pick, jnp.concatenate(returned, axis=0))
    return total.astype(BF), grad_gate[None], grad_up[None], grad_down[None]


def solution(mesh):
    fine = Mesh(mesh.devices.reshape(4, 4, 2, 4, 2), ("y", "x", "zh", "zl", "c"))
    tok = ("y", "x", "zh")
    cuts = ("zl", "c")
    hid = ("y", "zl", "c")
    return jax.shard_map(
        shards,
        mesh=fine,
        in_specs=(
            P(tok, cuts),
            P(tok, cuts),
            P(tok, None),
            P(tok, None),
            P(tok, None),
            P(tok, None),
            P(("x", "zh"), None, hid),
            P(("x", "zh"), None, hid),
            P(("x", "zh"), hid, None),
        ),
        out_specs=(
            P(tok, cuts),
            P(("x", "zh"), None, hid),
            P(("x", "zh"), None, hid),
            P(("x", "zh"), hid, None),
        ),
        check_vma=False,
    )
```

```python
import jax
import jax.numpy as jnp
from jax import lax
from jax.experimental import pallas as pl
from jax.experimental.pallas import tpu as pltpu
from jax.sharding import Mesh, PartitionSpec as P

TOPK = 2
BF = jnp.bfloat16
F32 = jnp.float32
SWAP = [(0, 1), (1, 0)]


def ring(step):
    return [(i, (i + step) % 4) for i in range(4)]


def zshift(flip, step):
    return [(h * 4 + l, (h ^ flip) * 4 + (l + step) % 4) for h in range(2) for l in range(4)]


def over_x(value, step):
    return lax.ppermute(value, "x", ring(step))


def over_y(value, step):
    return lax.ppermute(value, "y", ring(step))


def over_zl(value, step):
    return lax.ppermute(value, "zl", ring(step))


def over_z(value, flip, step):
    return lax.ppermute(value, ("zh", "zl"), zshift(flip, step))


def over_core(value):
    return lax.ppermute(value, "c", SWAP)


def dot(a, b):
    return jnp.dot(a, b, preferred_element_type=F32)


def dot_nt(a, b):
    return lax.dot_general(a, b, (((1,), (1,)), ((), ())), preferred_element_type=F32)


def dot_tn(a, b):
    return lax.dot_general(a, b, (((0,), (0,)), ((), ())), preferred_element_type=F32)


def rows_kernel(info_ref, *refs):
    near, far, grads = refs[:4], refs[4:8], refs[8:12]
    gate_ref, up_ref = refs[12:]
    cut = near[0].shape[1]
    units = gate_ref.shape[1]
    first = info_ref[1] == 0
    a = sum(dot_tn(near[r][...], grads[r][...]) for r in range(4))
    b = sum(dot_tn(far[r][...], grads[r][...]) for r in range(4))
    low = jnp.where(first, a, b).astype(BF)
    high = jnp.where(first, b, a).astype(BF)
    gate_ref[:cut, :] = low[:, :units]
    gate_ref[cut:, :] = high[:, :units]
    up_ref[:cut, :] = low[:, units:]
    up_ref[cut:, :] = high[:, units:]


def down_kernel(info_ref, *refs):
    near, far, hidden = refs[:4], refs[4:8], refs[8:12]
    down_ref = refs[12]
    cut = near[0].shape[1]
    first = info_ref[1] == 0
    a = sum(dot_tn(hidden[r][...], near[r][...]) for r in range(4))
    b = sum(dot_tn(hidden[r][...], far[r][...]) for r in range(4))
    down_ref[:, :cut] = jnp.where(first, a, b).astype(BF)
    down_ref[:, cut:] = jnp.where(first, b, a).astype(BF)


def weight_pass(kernel, info, near, far, factors, outs, by_rows):
    rows, columns = near[0].shape
    cut = columns // 4

    def turned(j, info_ref):
        place = (info_ref[0] + j) % 4
        return (place, 0) if by_rows else (0, place)

    row_specs = [pl.BlockSpec((rows, cut), lambda j, info_ref: (0, j))] * 8
    factor_specs = [pl.BlockSpec(f.shape, lambda j, info_ref: (0, 0)) for f in factors]
    blocks = [(s[0] // 4, s[1]) if by_rows else (s[0], s[1] // 4) for s in outs]
    width = factors[0].shape[1]
    return pl.pallas_call(
        kernel,
        grid_spec=pltpu.PrefetchScalarGridSpec(
            num_scalar_prefetch=1,
            grid=(4,),
            in_specs=row_specs + factor_specs,
            out_specs=[pl.BlockSpec(b, turned) for b in blocks],
        ),
        out_shape=[jax.ShapeDtypeStruct(s, BF) for s in outs],
        compiler_params=pltpu.CompilerParams(vmem_limit_bytes=32 * 1024 * 1024),
        cost_estimate=pl.CostEstimate(
            flops=2 * 4 * rows * 8 * cut * width, bytes_accessed=2 * 4 * rows * 8 * cut, transcendentals=0
        ),
    )(info, *near, *far, *factors)


def shards(tokens, cotangent, combine, expert_ids, slot_ids, keep_mask, w_gate, w_up, w_down):
    experts = 8
    tok_rows, cut = tokens.shape
    capacity = 9 * tok_rows * TOPK // (8 * experts)
    pair = 2 * capacity
    slots = experts * capacity
    units = w_gate.shape[2]
    half = 2 * cut
    x, zh = lax.axis_index("x"), lax.axis_index("zh")
    zl, c = lax.axis_index("zl"), lax.axis_index("c")
    info = jnp.stack([zl, c]).astype(jnp.int32)

    kept = keep_mask > 0
    target = ((expert_ids // 2 - x) % 4) * pair + (expert_ids % 2 != zh) * capacity + slot_ids
    target = jnp.where(kept, target, -1)
    positions = jnp.arange(slots, dtype=jnp.int32)
    routes = [positions[:, None] == target[:, k][None, :] for k in range(TOPK)]
    pick = (routes[0] | routes[1]).astype(BF)
    weight = sum(
        jnp.sum(jnp.where(routes[k], combine[:, k][None, :], 0.0), axis=1, keepdims=True)
        for k in range(TOPK)
    )
    both = dot(pick, jnp.concatenate([tokens, cotangent], axis=1))
    sent = jnp.concatenate([both[:, :cut], both[:, cut:] * weight], axis=1).astype(BF)
    got = [sent[:pair]] + [over_x(sent[s * pair : (s + 1) * pair], s) for s in range(1, 4)]
    got = jnp.stack(got).reshape(4, 2, capacity, 2 * cut)

    sides = [got[:, flip].reshape(slots // 2, 2 * cut) for flip in range(2)]
    own_rows = jnp.concatenate([sides[0], lax.ppermute(sides[1], "zh", SWAP)], axis=0)
    token_rows, scaled_rows = own_rows[:, :cut], own_rows[:, cut:]

    def turn_z(rows):
        return [rows] + [over_zl(rows, -j) for j in range(1, 4)]

    def from_sides(own):
        return over_y(own, -1), over_y(own, 1)

    def relayed(above, below):
        return over_y(below[:, :half], 1), over_y(above[:, half:], -1)

    pieces = turn_z(token_rows)
    w_gate, w_up, w_down, pieces[1] = lax.optimization_barrier((w_gate, w_up, w_down, pieces[1]))
    token_own = jnp.concatenate(pieces, axis=1)
    token_own, scaled_rows = lax.optimization_barrier((token_own, scaled_rows))
    scaled_own = jnp.concatenate(turn_z(scaled_rows), axis=1)

    joined = jnp.concatenate([w_gate[0], w_up[0]], axis=1).reshape(4, 2, cut, 2 * units)
    joined = jnp.concatenate([joined, joined[:3]], axis=0)

    down = w_down[0].reshape(units, 4, 2, cut)
    down = jnp.concatenate([down, down[:, :3]], axis=1)

    def turned(owner):
        rows = lax.dynamic_slice(joined, (zl, owner, 0, 0), (4, 1, cut, 2 * units))
        cols = lax.dynamic_slice(down, (0, zl, owner, 0), (units, 4, 1, cut))
        return rows.reshape(4 * cut, 2 * units), cols.reshape(units, 4 * cut)

    (near_w, near_down), (far_w, far_down) = turned(c), turned(1 - c)

    token_above, token_below = from_sides(token_own)
    token_across = relayed(token_above, token_below)
    scaled_above, scaled_below = from_sides(scaled_own)
    token_across, scaled_above, scaled_below = lax.optimization_barrier(
        (token_across, scaled_above, scaled_below)
    )
    scaled_across = relayed(scaled_above, scaled_below)
    token_near = [jnp.concatenate(token_across, axis=1), token_above, token_below, token_own]
    token_far = [over_core(v) for v in token_near]
    scaled_near = [None, scaled_above, scaled_below, scaled_own]
    scaled_far = [None] + [over_core(v) for v in scaled_near[1:]]
    grads, hidden = [None] * 4, [None] * 4

    def unit_pass(r):
        pre = dot(token_near[r], near_w) + dot(token_far[r], far_w)
        back_pre = dot_nt(scaled_near[r], near_down) + dot_nt(scaled_far[r], far_down)
        gate, up = pre[:, :units], pre[:, units:]
        squash = jax.nn.sigmoid(gate)
        active = gate * squash
        hidden[r] = (active * up).astype(BF)
        gate_grad = (back_pre * up * (squash * (1.0 + gate * (1.0 - squash)))).astype(BF)
        up_grad = (back_pre * active).astype(BF)
        grads[r] = jnp.concatenate([gate_grad, up_grad], axis=1)

    model = experts * cut

    def far_half(r):
        return dot_nt(grads[r], far_w).astype(BF)

    def halves(r, far_rows):
        got = over_core(far_rows).astype(F32)
        return (
            dot_nt(grads[r], near_w[:half]) + got[:, :half],
            dot_nt(grads[r], near_w[half:]) + got[:, half:],
        )

    unit_pass(1)
    unit_pass(2)
    far_above, far_below = far_half(1), far_half(2)
    scaled_across, far_above, far_below = lax.optimization_barrier((scaled_across, far_above, far_below))
    above, below = halves(1, far_above), halves(2, far_below)
    scaled_near[0] = jnp.concatenate(scaled_across, axis=1)
    scaled_far[0] = over_core(scaled_near[0])
    unit_pass(0)
    unit_pass(3)
    across = halves(0, far_half(0))
    across_a, across_b = across[0].astype(BF), across[1].astype(BF)
    relay_a = over_y(across_a, 1)
    relay_b = over_y(across_b, -1)
    later, across_a, across_b = lax.optimization_barrier((grads, across_a, across_b))
    grad_gate, grad_up = weight_pass(
        rows_kernel, info, token_near, token_far, later, [(model, units), (model, units)], True
    )
    below_a, above_b = below[0].astype(BF), above[1].astype(BF)
    relay_a, relay_b, below_a, above_b, grad_gate, grad_up = lax.optimization_barrier(
        (relay_a, relay_b, below_a, above_b, grad_gate, grad_up)
    )

    from_below_a = over_y((above[0] + relay_a.astype(F32)).astype(BF), 1)
    from_above_a = over_y(below_a, -1)
    below_b = (below[1] + relay_b.astype(F32)).astype(BF)
    own = halves(3, far_half(3))
    (grad_down,) = weight_pass(
        down_kernel, info, scaled_near, scaled_far, hidden, [(units, model)], False
    )
    from_below_b = over_y(above_b, 1)
    from_above_b = over_y(below_b, -1)
    from_below_a, from_above_a, grad_down = lax.optimization_barrier(
        (from_below_a, from_above_a, grad_down)
    )

    def home(rows, flip, j):
        column = j % 2 * cut
        piece = rows[flip * slots // 2 : (flip + 1) * slots // 2, column : column + cut]
        return over_z(piece, flip, j) if flip or j else piece

    rows = (own[0] + from_below_a.astype(F32) + from_above_a.astype(F32)).astype(BF)
    other_home = [home(rows, 1, j) for j in range(2)]
    own_home = [home(rows, 0, j) for j in range(2)]
    from_below_b, from_above_b, own_home[1] = lax.optimization_barrier(
        (from_below_b, from_above_b, own_home[1])
    )
    rows = (own[1] + from_below_b.astype(F32) + from_above_b.astype(F32)).astype(BF)
    other_home += [home(rows, 1, j) for j in range(2, 4)]
    own_home += [home(rows, 0, j) for j in range(2, 4)]
    other_home, own_home[1] = lax.optimization_barrier((other_home, own_home[1]))
    other_sum = sum(v.astype(F32) for v in other_home).astype(BF)
    sums = [sum(v.astype(F32) for v in own_home).astype(BF), other_sum]
    place = positions // pair * capacity + positions % pair // capacity * (slots // 2) + positions % capacity
    order = (place[:, None] == positions[None, :]).astype(BF)
    sums = dot(order, jnp.concatenate(sums, axis=0)).astype(BF)
    returned = [sums[:pair]] + [over_x(sums[s * pair : (s + 1) * pair], -s) for s in range(1, 4)]
    total = dot_tn(pick, jnp.concatenate(returned, axis=0))
    return total.astype(BF), grad_gate[None], grad_up[None], grad_down[None]


def solution(mesh):
    fine = Mesh(mesh.devices.reshape(4, 4, 2, 4, 2), ("y", "x", "zh", "zl", "c"))
    tok = ("y", "x", "zh")
    cuts = ("zl", "c")
    hid = ("y", "zl", "c")
    return jax.shard_map(
        shards,
        mesh=fine,
        in_specs=(
            P(tok, cuts),
            P(tok, cuts),
            P(tok, None),
            P(tok, None),
            P(tok, None),
            P(tok, None),
            P(("x", "zh"), None, hid),
            P(("x", "zh"), None, hid),
            P(("x", "zh"), hid, None),
        ),
        out_specs=(
            P(tok, cuts),
            P(("x", "zh"), None, hid),
            P(("x", "zh"), None, hid),
            P(("x", "zh"), hid, None),
        ),
        check_vma=False,
    )
```

```python
import jax
import jax.numpy as jnp
from jax import lax
from jax.experimental import pallas as pl
from jax.experimental.pallas import tpu as pltpu
from jax.sharding import Mesh, PartitionSpec as P

TOPK = 2
BF = jnp.bfloat16
F32 = jnp.float32
SWAP = [(0, 1), (1, 0)]


def ring(step):
    return [(i, (i + step) % 4) for i in range(4)]


def zshift(flip, step):
    return [(h * 4 + l, (h ^ flip) * 4 + (l + step) % 4) for h in range(2) for l in range(4)]


def over_x(value, step):
    return lax.ppermute(value, "x", ring(step))


def over_y(value, step):
    return lax.ppermute(value, "y", ring(step))


def over_zl(value, step):
    return lax.ppermute(value, "zl", ring(step))


def over_z(value, flip, step):
    return lax.ppermute(value, ("zh", "zl"), zshift(flip, step))


def over_core(value):
    return lax.ppermute(value, "c", SWAP)


def dot(a, b):
    return jnp.dot(a, b, preferred_element_type=F32)


def dot_nt(a, b):
    return lax.dot_general(a, b, (((1,), (1,)), ((), ())), preferred_element_type=F32)


def dot_tn(a, b):
    return lax.dot_general(a, b, (((0,), (0,)), ((), ())), preferred_element_type=F32)


def rows_kernel(info_ref, *refs):
    near, far, grads = refs[:4], refs[4:8], refs[8:12]
    gate_ref, up_ref = refs[12:]
    cut = near[0].shape[1]
    units = gate_ref.shape[1]
    first = info_ref[1] == 0
    a = sum(dot_tn(near[r][...], grads[r][...]) for r in range(4))
    b = sum(dot_tn(far[r][...], grads[r][...]) for r in range(4))
    low = jnp.where(first, a, b).astype(BF)
    high = jnp.where(first, b, a).astype(BF)
    gate_ref[:cut, :] = low[:, :units]
    gate_ref[cut:, :] = high[:, :units]
    up_ref[:cut, :] = low[:, units:]
    up_ref[cut:, :] = high[:, units:]


def down_kernel(info_ref, *refs):
    near, far, hidden = refs[:4], refs[4:8], refs[8:12]
    down_ref = refs[12]
    cut = near[0].shape[1]
    first = info_ref[1] == 0
    a = sum(dot_tn(hidden[r][...], near[r][...]) for r in range(4))
    b = sum(dot_tn(hidden[r][...], far[r][...]) for r in range(4))
    down_ref[:, :cut] = jnp.where(first, a, b).astype(BF)
    down_ref[:, cut:] = jnp.where(first, b, a).astype(BF)


def weight_pass(kernel, info, near, far, factors, outs, by_rows):
    rows, columns = near[0].shape
    cut = columns // 4

    def turned(j, info_ref):
        place = (info_ref[0] + j) % 4
        return (place, 0) if by_rows else (0, place)

    row_specs = [pl.BlockSpec((rows, cut), lambda j, info_ref: (0, j))] * 8
    factor_specs = [pl.BlockSpec(f.shape, lambda j, info_ref: (0, 0)) for f in factors]
    blocks = [(s[0] // 4, s[1]) if by_rows else (s[0], s[1] // 4) for s in outs]
    width = factors[0].shape[1]
    return pl.pallas_call(
        kernel,
        grid_spec=pltpu.PrefetchScalarGridSpec(
            num_scalar_prefetch=1,
            grid=(4,),
            in_specs=row_specs + factor_specs,
            out_specs=[pl.BlockSpec(b, turned) for b in blocks],
        ),
        out_shape=[jax.ShapeDtypeStruct(s, BF) for s in outs],
        compiler_params=pltpu.CompilerParams(vmem_limit_bytes=32 * 1024 * 1024),
        cost_estimate=pl.CostEstimate(
            flops=2 * 4 * rows * 8 * cut * width, bytes_accessed=2 * 4 * rows * 8 * cut, transcendentals=0
        ),
    )(info, *near, *far, *factors)


def shards(tokens, cotangent, combine, expert_ids, slot_ids, keep_mask, w_gate, w_up, w_down):
    experts = 8
    tok_rows, cut = tokens.shape
    capacity = 9 * tok_rows * TOPK // (8 * experts)
    pair = 2 * capacity
    slots = experts * capacity
    units = w_gate.shape[2]
    half = 2 * cut
    x, zh = lax.axis_index("x"), lax.axis_index("zh")
    zl, c = lax.axis_index("zl"), lax.axis_index("c")
    info = jnp.stack([zl, c]).astype(jnp.int32)

    kept = keep_mask > 0
    target = ((expert_ids // 2 - x) % 4) * pair + (expert_ids % 2 != zh) * capacity + slot_ids
    target = jnp.where(kept, target, -1)
    positions = jnp.arange(slots, dtype=jnp.int32)
    routes = [positions[:, None] == target[:, k][None, :] for k in range(TOPK)]
    pick = (routes[0] | routes[1]).astype(BF)
    weight = sum(
        jnp.sum(jnp.where(routes[k], combine[:, k][None, :], 0.0), axis=1, keepdims=True)
        for k in range(TOPK)
    )
    both = dot(pick, jnp.concatenate([tokens, cotangent], axis=1))
    sent = jnp.concatenate([both[:, :cut], both[:, cut:] * weight], axis=1).astype(BF)
    got = [sent[:pair]] + [over_x(sent[s * pair : (s + 1) * pair], s) for s in range(1, 4)]
    got = jnp.stack(got).reshape(4, 2, capacity, 2 * cut)

    sides = [got[:, flip].reshape(slots // 2, 2 * cut) for flip in range(2)]
    own_rows = jnp.concatenate([sides[0], lax.ppermute(sides[1], "zh", SWAP)], axis=0)
    token_rows, scaled_rows = own_rows[:, :cut], own_rows[:, cut:]

    def turn_z(rows):
        return [rows] + [over_zl(rows, -j) for j in range(1, 4)]

    def from_sides(own):
        return over_y(own, -1), over_y(own, 1)

    def relayed(above, below):
        return over_y(below[:, :half], 1), over_y(above[:, half:], -1)

    pieces = turn_z(token_rows)
    token_own = jnp.concatenate(pieces, axis=1)
    token_own, scaled_rows = lax.optimization_barrier((token_own, scaled_rows))
    pieces = turn_z(scaled_rows)
    w_gate, w_up, w_down, pieces[1], pieces[3] = lax.optimization_barrier(
        (w_gate, w_up, w_down, pieces[1], pieces[3])
    )
    scaled_own = jnp.concatenate(pieces, axis=1)

    joined = jnp.concatenate([w_gate[0], w_up[0]], axis=1).reshape(4, 2, cut, 2 * units)
    joined = jnp.concatenate([joined, joined[:3]], axis=0)

    down = w_down[0].reshape(units, 4, 2, cut)
    down = jnp.concatenate([down, down[:, :3]], axis=1)

    def turned(owner):
        rows = lax.dynamic_slice(joined, (zl, owner, 0, 0), (4, 1, cut, 2 * units))
        cols = lax.dynamic_slice(down, (0, zl, owner, 0), (units, 4, 1, cut))
        return rows.reshape(4 * cut, 2 * units), cols.reshape(units, 4 * cut)

    (near_w, near_down), (far_w, far_down) = turned(c), turned(1 - c)

    token_above, token_below = from_sides(token_own)
    token_across = relayed(token_above, token_below)
    scaled_above, scaled_below = from_sides(scaled_own)
    token_across, scaled_above, scaled_below = lax.optimization_barrier(
        (token_across, scaled_above, scaled_below)
    )
    scaled_across = relayed(scaled_above, scaled_below)
    token_near = [jnp.concatenate(token_across, axis=1), token_above, token_below, token_own]
    token_far = [over_core(v) for v in token_near]
    scaled_near = [None, scaled_above, scaled_below, scaled_own]
    scaled_far = [None] + [over_core(v) for v in scaled_near[1:]]
    grads, hidden = [None] * 4, [None] * 4

    def unit_pass(r):
        pre = dot(token_near[r], near_w) + dot(token_far[r], far_w)
        back_pre = dot_nt(scaled_near[r], near_down) + dot_nt(scaled_far[r], far_down)
        gate, up = pre[:, :units], pre[:, units:]
        squash = jax.nn.sigmoid(gate)
        active = gate * squash
        hidden[r] = (active * up).astype(BF)
        gate_grad = (back_pre * up * (squash * (1.0 + gate * (1.0 - squash)))).astype(BF)
        up_grad = (back_pre * active).astype(BF)
        grads[r] = jnp.concatenate([gate_grad, up_grad], axis=1)

    model = experts * cut

    def far_half(r):
        return dot_nt(grads[r], far_w).astype(BF)

    def halves(r, far_rows):
        got = over_core(far_rows).astype(F32)
        return (
            dot_nt(grads[r], near_w[:half]) + got[:, :half],
            dot_nt(grads[r], near_w[half:]) + got[:, half:],
        )

    unit_pass(1)
    unit_pass(2)
    far_above, far_below = far_half(1), far_half(2)
    scaled_across, far_above, far_below = lax.optimization_barrier((scaled_across, far_above, far_below))
    above, below = halves(1, far_above), halves(2, far_below)
    scaled_near[0] = jnp.concatenate(scaled_across, axis=1)
    scaled_far[0] = over_core(scaled_near[0])
    unit_pass(0)
    unit_pass(3)
    across = halves(0, far_half(0))
    across_a, across_b = across[0].astype(BF), across[1].astype(BF)
    relay_a = over_y(across_a, 1)
    relay_b = over_y(across_b, -1)
    later, across_a, across_b = lax.optimization_barrier((grads, across_a, across_b))
    grad_gate, grad_up = weight_pass(
        rows_kernel, info, token_near, token_far, later, [(model, units), (model, units)], True
    )
    below_a, above_b = below[0].astype(BF), above[1].astype(BF)
    relay_a, relay_b, below_a, above_b, grad_gate, grad_up = lax.optimization_barrier(
        (relay_a, relay_b, below_a, above_b, grad_gate, grad_up)
    )

    from_below_a = over_y((above[0] + relay_a.astype(F32)).astype(BF), 1)
    from_above_a = over_y(below_a, -1)
    below_b = (below[1] + relay_b.astype(F32)).astype(BF)
    own = halves(3, far_half(3))
    (grad_down,) = weight_pass(
        down_kernel, info, scaled_near, scaled_far, hidden, [(units, model)], False
    )
    from_below_b = over_y(above_b, 1)
    from_above_b = over_y(below_b, -1)
    from_below_a, from_above_a, grad_down = lax.optimization_barrier(
        (from_below_a, from_above_a, grad_down)
    )

    def home(rows, flip, j):
        column = j % 2 * cut
        piece = rows[flip * slots // 2 : (flip + 1) * slots // 2, column : column + cut]
        return over_z(piece, flip, j) if flip or j else piece

    rows = (own[0] + from_below_a.astype(F32) + from_above_a.astype(F32)).astype(BF)
    other_home = [home(rows, 1, j) for j in range(2)]
    own_home = [home(rows, 0, j) for j in range(2)]
    from_below_b, from_above_b, own_home[1] = lax.optimization_barrier(
        (from_below_b, from_above_b, own_home[1])
    )
    rows = (own[1] + from_below_b.astype(F32) + from_above_b.astype(F32)).astype(BF)
    other_home += [home(rows, 1, j) for j in range(2, 4)]
    own_home += [home(rows, 0, j) for j in range(2, 4)]
    other_home, own_home[1] = lax.optimization_barrier((other_home, own_home[1]))
    other_sum = sum(v.astype(F32) for v in other_home).astype(BF)
    sums = [sum(v.astype(F32) for v in own_home).astype(BF), other_sum]
    place = positions // pair * capacity + positions % pair // capacity * (slots // 2) + positions % capacity
    order = (place[:, None] == positions[None, :]).astype(BF)
    sums = dot(order, jnp.concatenate(sums, axis=0)).astype(BF)
    returned = [sums[:pair]] + [over_x(sums[s * pair : (s + 1) * pair], -s) for s in range(1, 4)]
    total = dot_tn(pick, jnp.concatenate(returned, axis=0))
    return total.astype(BF), grad_gate[None], grad_up[None], grad_down[None]


def solution(mesh):
    fine = Mesh(mesh.devices.reshape(4, 4, 2, 4, 2), ("y", "x", "zh", "zl", "c"))
    tok = ("y", "x", "zh")
    cuts = ("zl", "c")
    hid = ("y", "zl", "c")
    return jax.shard_map(
        shards,
        mesh=fine,
        in_specs=(
            P(tok, cuts),
            P(tok, cuts),
            P(tok, None),
            P(tok, None),
            P(tok, None),
            P(tok, None),
            P(("x", "zh"), None, hid),
            P(("x", "zh"), None, hid),
            P(("x", "zh"), hid, None),
        ),
        out_specs=(
            P(tok, cuts),
            P(("x", "zh"), None, hid),
            P(("x", "zh"), None, hid),
            P(("x", "zh"), hid, None),
        ),
        check_vma=False,
    )
```
